32 devices in a mesh: det: 4 (over z), tm: 8 (over y, x, core).
Axes of the slice: x: 2, y: 2, z: 4, core: 2. Of those that a mesh axis runs over, the one named last changes fastest.
Arguments:
- iterate: float32 [16, 262144], P(None, ('det', 'tm')), may hold values from -6 to 6
- residual: float32 [16, 262144], P(None, ('det', 'tm')), may hold values from -40 to 40
- direction: float32 [16, 262144], P(None, ('det', 'tm')), may hold values from -2.5 to 2.5
- precond: float32 [262144], P(('det', 'tm')), may hold values from 0.02 to 0.12
- patch_ids: int32 [128, 64], P('det', 'tm'), may hold values from 0 to 4095, as said below
- pixel_in: int32 [128, 8192], P('det', 'tm'), may hold values from 0 to 63
- weights: float32 [128, 8192], P('det', 'tm'), may hold values from 0.5 to 1.5
- filter_diag: float32 [128], P('det'), may hold values from 1 to 1.5
- filter_band: float32 [128, 64], P('det'), may hold values from 0.003125 to 0.0075
Outputs:
- new_iterate: float32 [16, 262144], P(None, ('det', 'tm'))
- new_residual: float32 [16, 262144], P(None, ('det', 'tm'))
- new_direction: float32 [16, 262144], P(None, ('det', 'tm'))
The draws below stay inside these ranges and needn't reach their ends.
Inputs may be any that keep to these rules, and one draw needn't show every extreme that they name: `patch_ids`: the blocks of one device (detectors 32 d0 .. and time blocks 8 t0 .. of its det index a and tm index c) name, for every owner o = a2 * 8 + c2, exactly 8 patches p with p // 128 = o.
All inputs are finite; a program needn't handle non-finite values.
Results may differ from the reference program's by a relative error of at most 0.0003.
Values sent between devices are 32-bit elements; how exact they have to be, the bound alone decides.
A program may use at most 64 MiB of HBM per device.

```python
import math
import jax
import jax.numpy as jnp
from jax import lax

PROBES = 16
SB = 128
PX = 64
ND_DEV = 32
PATCH_DEV = 128
H = 64
TB_DEV = 8
BLK_DEV = 256
PER_OWNER = 8
DGROUPS = 4
SPANS = 8
DETS = 128
TSAMP = 8192
TBLK = 64
NPIX = 262144
DEVICES = 32


def rising_field(key, level, limit):
    position = jnp.arange(NPIX, dtype=jnp.float32) / NPIX
    values = jax.random.normal(key, (PROBES, NPIX), jnp.float32) * level * (1.0 + position)[None, :]
    return jnp.clip(values, -limit, limit)


def draw_residual(key, part):
    return rising_field(jax.random.fold_in(key, 11), 4.0, 40.0)


def draw_direction(key, part):
    return rising_field(jax.random.fold_in(key, 23), 0.25, 2.5)


def draw_patch_ids(key, part):

    def one_device(device_index):
        dev_key = jax.random.fold_in(key, device_index)
        perm_key, off_key = jax.random.split(dev_key)
        owners = jnp.arange(BLK_DEV, dtype=jnp.int32) // PER_OWNER
        owners = jax.random.permutation(perm_key, owners)
        offset = jax.random.randint(off_key, (BLK_DEV,), 0, PATCH_DEV, dtype=jnp.int32)
        return owners * PATCH_DEV + offset
    blocks_all = jax.vmap(one_device)(jnp.arange(DEVICES, dtype=jnp.int32))
    blocks_all = blocks_all.reshape(DGROUPS, SPANS, ND_DEV, TB_DEV).transpose(0, 2, 1, 3)
    return blocks_all.reshape(DETS, TBLK).astype(jnp.int32)


def touch_ends(drawn, key, smallest, high):
    extent = drawn.shape
    place = [jax.random.randint(jax.random.fold_in(key, axis), (), 0, extent[axis]) for axis in range(len(extent))]
    drawn = drawn.at[tuple(place)].set(smallest)
    longest = extent.index(max(extent))
    place[longest] = (place[longest] + 1) % extent[longest]
    return drawn.at[tuple(place)].set(high)


def levels(rng, extent, pieces, low, top_value):
    factor_of = 1.0
    for axis_at, parts in pieces:
        heights = jax.random.uniform(jax.random.fold_in(jax.random.fold_in(rng, 6), axis_at), (parts,), jnp.float32, low / len(pieces), top_value / len(pieces))
        factor_of = factor_of * jnp.repeat(jnp.exp(heights), extent[axis_at] // parts).reshape((-1,) + (1,) * (len(extent) - 1 - axis_at))
    return factor_of


def gaussian(stream_key, shape, deviation, bound, pieces=(), held_as=jnp.bfloat16):
    gain = levels(stream_key, shape, pieces, -0.22, 0.18) if pieces else 1.0
    array = jax.random.normal(stream_key, shape, jnp.float32) * deviation * gain
    return jnp.minimum(jnp.maximum(array, -bound), bound).astype(held_as)


def setup_inputs(seed: int = 0) -> dict:
    keys = jax.random.split(jax.random.key(seed), 10)
    iterate = gaussian(keys[0], (PROBES, NPIX), 1.0, 6.0, ((1, 32),), jnp.float32)
    residual = draw_residual(jax.random.fold_in(keys[9], 71), 0)
    direction = draw_direction(jax.random.fold_in(keys[9], 71), 0)
    precond = jnp.clip(jnp.exp(math.log(0.12) - 1.7917595 * jax.random.uniform(keys[3], (NPIX,), jnp.float32) ** levels(keys[3], (NPIX,), ((0, 32),), -0.2, 0.2)), 0.02, 0.12)
    patch_ids = draw_patch_ids(jax.random.fold_in(keys[9], 71), 0)
    pixel_in = touch_ends(jax.random.randint(keys[5], (DETS, TSAMP), 0, PX), jax.random.fold_in(keys[5], 1), 0, PX - 1).astype(jnp.int32)
    weights = jnp.clip(0.5 + 1.0 * jax.random.uniform(keys[6], (DETS, TSAMP), jnp.float32) ** levels(keys[6], (DETS, TSAMP), ((0, 4), (1, 8)), -0.2, 0.2), 0.5, 1.5)
    filter_diag = jnp.clip(1.0 + 0.5 * jax.random.uniform(keys[7], (DETS,), jnp.float32) ** levels(keys[7], (DETS,), ((0, 4),), -0.2, 0.2), 1.0, 1.5)
    filter_band = jnp.clip(0.003125 + 0.004374999785795808 * jax.random.uniform(keys[8], (DETS, H), jnp.float32) ** levels(keys[8], (DETS, H), ((0, 4),), -0.2, 0.2), 0.003125, 0.0075)
    return dict(iterate=iterate, residual=residual, direction=direction, precond=precond, patch_ids=patch_ids, pixel_in=pixel_in, weights=weights, filter_diag=filter_diag, filter_band=filter_band)


def toeplitz_blocks(filter_diag, filter_band):
    half_band = filter_band.shape[1]
    block_len = 2 * half_band
    coeffs = jnp.concatenate([filter_diag[:, None], filter_band], axis=1)
    offsets = jnp.abs(jnp.arange(2 * block_len, dtype=jnp.int32)[:, None] - jnp.arange(block_len, dtype=jnp.int32)[None, :] - half_band)
    band_hot = (offsets[:, :, None] == jnp.arange(half_band + 1, dtype=jnp.int32)[None, None, :]).astype(jnp.float32)
    return jnp.einsum('usk,dk->dus', band_hot, coeffs, precision=lax.Precision.HIGHEST)


def reference(iterate, residual, direction, precond, patch_ids, pixel_in, weights, filter_diag, filter_band):
    norm_old = jnp.sum(residual * precond * residual, axis=1)
    toeplitz = toeplitz_blocks(filter_diag, filter_band)
    patch_groups = patch_ids.reshape(DGROUPS, ND_DEV, TBLK)
    pixel_groups = pixel_in.reshape(DGROUPS, ND_DEV, TSAMP)
    gain_groups = weights.reshape(DGROUPS, ND_DEV, TSAMP)
    toep_groups = toeplitz.reshape(DGROUPS, ND_DEV, 2 * SB, SB)

    def one_group(image_map, inputs):
        patch_rows, pixel_rows, gain_rows, toep_rows = inputs
        global_px = (jnp.repeat(patch_rows, SB, axis=1) * PX + pixel_rows).astype(jnp.int32)
        timeline = direction[:, global_px] * gain_rows[None]
        padded = jnp.pad(timeline, ((0, 0), (0, 0), (H, H)))
        windows = jnp.concatenate([
            padded[:, :, :TSAMP].reshape(PROBES, ND_DEV, TBLK, SB),
            padded[:, :, SB:TSAMP + SB].reshape(PROBES, ND_DEV, TBLK, SB)], axis=3)
        filtered = jnp.einsum('pdju,dus->pdjs', windows, toep_rows, precision=lax.Precision.HIGHEST)
        weighted = filtered.reshape(PROBES, ND_DEV, TSAMP) * gain_rows[None]
        added = jax.ops.segment_sum(weighted.reshape(PROBES, -1).T, global_px.reshape(-1), num_segments=NPIX).T
        return image_map + added, jnp.zeros((), jnp.float32)

    image_map = lax.scan(one_group, jnp.zeros((PROBES, NPIX), jnp.float32), (patch_groups, pixel_groups, gain_groups, toep_groups))[0]
    curvature = jnp.sum(direction * image_map, axis=1)
    step_size = norm_old / curvature
    new_iterate = iterate + step_size[:, None] * direction
    new_residual = residual - step_size[:, None] * image_map
    scaled = precond * new_residual
    norm_new = jnp.sum(new_residual * scaled, axis=1)
    new_direction = scaled + (norm_new / norm_old)[:, None] * direction
    return (new_iterate, new_residual, new_direction)
```

```python
import functools

import jax
import jax.numpy as jnp
from jax import lax
from jax.experimental import pallas as pl
from jax.experimental.pallas import tpu as pltpu
from jax.sharding import PartitionSpec as P

PX = 64


def with_halo(cells, sides, width):
    for axis, dim in sides:
        count = lax.axis_size(axis)
        ends = count - 1
        head = lax.slice_in_dim(cells, 0, width, axis=dim)
        tail = lax.slice_in_dim(cells, cells.shape[dim] - width, cells.shape[dim], axis=dim)
        cells = jnp.concatenate(
            [
                lax.ppermute(tail, axis, [(i, (i + 1) % count) for i in range(ends)]),
                cells,
                lax.ppermute(head, axis, [((i + 1) % count, i) for i in range(ends)]),
            ],
            axis=dim,
        )
    return cells


def share_kernel(spans, devices, part_ref, out_ref, held, send_sem, recv_sem):
    me = lax.axis_index("det") * spans + lax.axis_index("tm")
    barrier = pltpu.get_barrier_semaphore()

    def place(step):
        peer = lax.rem(me + step, devices)
        return (peer // spans, lax.rem(peer, spans))

    def copy_to(step):
        return pltpu.make_async_remote_copy(
            src_ref=part_ref,
            dst_ref=held.at[step],
            send_sem=send_sem.at[step],
            recv_sem=recv_sem.at[step],
            device_id=place(step),
            device_id_type=pl.DeviceIdType.MESH,
        )

    @pl.loop(1, devices)
    def _(step):
        pl.semaphore_signal(
            barrier, inc=1, device_id=place(step), device_id_type=pl.DeviceIdType.MESH
        )

    pl.semaphore_wait(barrier, devices - 1)

    @pl.loop(1, devices)
    def _(step):
        copy_to(step).start()

    held[0] = part_ref[...]

    @pl.loop(1, devices)
    def _(step):
        copy_to(step).wait()

    out_ref[...] = jnp.sum(held[...], axis=0)


def sum_everywhere(part, spans, devices):
    return pl.pallas_call(
        functools.partial(share_kernel, spans, devices),
        out_shape=jax.ShapeDtypeStruct(part.shape, jnp.float32),
        in_specs=[pl.BlockSpec(memory_space=pltpu.VMEM)],
        out_specs=pl.BlockSpec(memory_space=pltpu.VMEM),
        scratch_shapes=[
            pltpu.VMEM((devices,) + part.shape, jnp.float32),
            pltpu.SemaphoreType.DMA((devices,)),
            pltpu.SemaphoreType.DMA((devices,)),
        ],
        compiler_params=pltpu.CompilerParams(collective_id=0, has_side_effects=True),
    )(part)


def per_device(
    iterate, residual, direction, precond, patch_ids, pixel_in, weights, filter_diag, filter_band
):
    probes = iterate.shape[0]
    det_rows, time_blocks = patch_ids.shape
    samples = pixel_in.shape[1]
    block_len = samples // time_blocks
    half_band = filter_band.shape[1]
    groups = lax.axis_size("det")
    spans = lax.axis_size("tm")
    devices = groups * spans
    blocks = det_rows * time_blocks
    per_owner = blocks // devices
    own_patches = iterate.shape[1] // PX
    width = probes * PX
    patch_flat = patch_ids.reshape(blocks)
    owners = patch_flat // own_patches
    sort_order = jnp.argsort(owners, stable=True)
    inverse = jnp.argsort(sort_order, stable=True)
    requests = (patch_flat[sort_order] % own_patches).reshape(devices, per_owner)
    asked_rows = lax.all_to_all(requests, ("det", "tm"), split_axis=0, concat_axis=0, tiled=True)
    asked_hot = (
        asked_rows.reshape(-1)[:, None] == jnp.arange(own_patches, dtype=jnp.int32)[None, :]
    ).astype(jnp.float32)
    patch_table = (
        direction.reshape(probes, own_patches, PX).transpose(1, 0, 2).reshape(own_patches, width)
    )
    served = jnp.dot(asked_hot, patch_table, precision=lax.Precision.HIGHEST).reshape(
        devices, per_owner, width
    )
    fetched = lax.all_to_all(served, ("det", "tm"), split_axis=0, concat_axis=0, tiled=True)
    block_vals = fetched.reshape(blocks, width)[inverse].reshape(blocks, probes, PX)
    pixel_hot = (
        pixel_in.reshape(blocks, block_len)[:, :, None]
        == jnp.arange(PX, dtype=jnp.int32)[None, None, :]
    ).astype(jnp.float32)
    sample_gain = weights.reshape(blocks, block_len)
    timeline = (
        jnp.einsum("bpx,bsx->bps", block_vals, pixel_hot, precision=lax.Precision.HIGHEST)
        * sample_gain[:, None, :]
    )
    timeline = (
        timeline.reshape(det_rows, time_blocks, probes, block_len)
        .transpose(2, 0, 1, 3)
        .reshape(probes, det_rows, samples)
    )
    padded = with_halo(timeline, (("tm", 2),), half_band)
    windows = jnp.concatenate(
        [
            padded[:, :, :samples].reshape(probes, det_rows, time_blocks, block_len),
            padded[:, :, block_len : samples + block_len].reshape(
                probes, det_rows, time_blocks, block_len
            ),
        ],
        axis=3,
    )
    coeffs = jnp.concatenate([filter_diag[:, None], filter_band], axis=1)
    offsets = jnp.abs(
        jnp.arange(2 * block_len, dtype=jnp.int32)[:, None]
        - jnp.arange(block_len, dtype=jnp.int32)[None, :]
        - half_band
    )
    band_hot = (
        offsets[:, :, None] == jnp.arange(half_band + 1, dtype=jnp.int32)[None, None, :]
    ).astype(jnp.float32)
    toeplitz = jnp.einsum("usk,dk->dus", band_hot, coeffs, precision=lax.Precision.HIGHEST)
    filtered = jnp.einsum("pdju,dus->pdjs", windows, toeplitz, precision=lax.Precision.HIGHEST)
    weighted = (
        filtered.transpose(1, 2, 0, 3).reshape(blocks, probes, block_len) * sample_gain[:, None, :]
    )
    partial_value = jnp.einsum(
        "bps,bsx->bpx", weighted, pixel_hot, precision=lax.Precision.HIGHEST
    ).reshape(blocks, width)
    partial_value = partial_value[sort_order].reshape(devices, per_owner, width)
    collected = lax.all_to_all(
        partial_value, ("det", "tm"), split_axis=0, concat_axis=0, tiled=True
    )
    collected = collected.reshape(devices * per_owner, width)
    summed = lax.dot_general(
        asked_hot, collected, (((0,), (0,)), ((), ())), precision=lax.Precision.HIGHEST
    )
    image_map = (
        summed.reshape(own_patches, probes, PX).transpose(1, 0, 2).reshape(probes, own_patches * PX)
    )
    lean = precond * residual
    drop = precond * image_map
    sums = jnp.stack(
        [
            jnp.sum(residual * lean, axis=1),
            jnp.sum(direction * image_map, axis=1),
            jnp.sum(image_map * lean, axis=1),
            jnp.sum(image_map * drop, axis=1),
        ]
    )
    part = jnp.pad(sums, ((0, 4), (0, 128 - probes)))
    total = sum_everywhere(part, spans, devices)
    norm_old, curvature, cross, square = (total[i, :probes] for i in range(4))
    step_size = norm_old / curvature
    norm_new = norm_old - step_size * (2.0 * cross - step_size * square)
    new_iterate = iterate + step_size[:, None] * direction
    new_residual = residual - step_size[:, None] * image_map
    scaled = precond * new_residual
    new_direction = scaled + (norm_new / norm_old)[:, None] * direction
    return (new_iterate, new_residual, new_direction)


def solution(mesh):
    in_specs = (
        P(None, ("det", "tm")),
        P(None, ("det", "tm")),
        P(None, ("det", "tm")),
        P(("det", "tm")),
        P("det", "tm"),
        P("det", "tm"),
        P("det", "tm"),
        P("det"),
        P("det", None),
    )
    out_specs = (P(None, ("det", "tm")), P(None, ("det", "tm")), P(None, ("det", "tm")))
    return jax.shard_map(
        per_device, mesh=mesh, in_specs=in_specs, out_specs=out_specs, check_vma=False
    )
```

```python
import functools

import jax
import jax.numpy as jnp
from jax import lax
from jax.experimental import pallas as pl
from jax.experimental.pallas import tpu as pltpu
from jax.sharding import PartitionSpec as P

PX = 64


def halves(values):
    top = values.astype(jnp.bfloat16)
    return top, (values - top.astype(jnp.float32)).astype(jnp.bfloat16)


def vmem(count):
    return [pl.BlockSpec(memory_space=pltpu.VMEM)] * count


def smem():
    return pl.BlockSpec(memory_space=pltpu.SMEM)


def serve_kernel(asked_ref, table_ref, out_ref):
    @pl.loop(0, out_ref.shape[0], step=8)
    def _(first):
        for i in range(8):
            out_ref[first + i] = table_ref[asked_ref[first + i]]


def serve(asked, table):
    return pl.pallas_call(
        serve_kernel,
        out_shape=jax.ShapeDtypeStruct(asked.shape + table.shape[1:], jnp.float32),
        in_specs=[smem()] + vmem(1),
        out_specs=vmem(1)[0],
    )(asked, table)


def gather_up_kernel(asked_ref, parts_ref, out_ref):
    out_ref[...] = jnp.zeros_like(out_ref)

    @pl.loop(0, parts_ref.shape[0], step=8)
    def _(first):
        for i in range(8):
            row = asked_ref[first + i]
            out_ref[row] = out_ref[row] + parts_ref[first + i]


def gather_up(asked, parts, rows):
    return pl.pallas_call(
        gather_up_kernel,
        out_shape=jax.ShapeDtypeStruct((rows,) + parts.shape[1:], jnp.float32),
        in_specs=[smem()] + vmem(1),
        out_specs=vmem(1)[0],
    )(asked, parts)


def scan_kernel(slot_ref, patches_ref, pixel_ref, gain_ref, line_ref, head_ref, tail_ref):
    rows, blocks, _ = pixel_ref.shape
    half = rows // 2
    left = lax.broadcasted_iota(jnp.int32, (16, 128), 1) < 64

    def one_row(d):
        pixels, gains = pixel_ref[d], gain_ref[d]
        for j in range(blocks):
            pixel = jnp.broadcast_to(pixels[j : j + 1], (8, 128))
            gain = jnp.broadcast_to(gains[j : j + 1], (8, 128))
            patch = patches_ref[slot_ref[d * blocks + j]]
            line_ref[d, 16 * j : 16 * j + 8] = (
                jnp.take_along_axis(patch, pixel, axis=1) * gain
            )
            line_ref[d, 16 * j + 8 : 16 * j + 16] = (
                jnp.take_along_axis(patch, pixel + 64, axis=1) * gain
            )

    @pl.loop(0, half)
    def _(d):
        one_row(d)
        one_row(d + half)
        last = 16 * (blocks - 1)
        head_ref[d] = jnp.where(
            left, line_ref[d, 0:16], pltpu.roll(line_ref[d + half, 0:16], 64, 1)
        )
        tail_ref[d] = jnp.where(
            left,
            pltpu.roll(line_ref[d + half, last : last + 16], 64, 1),
            line_ref[d, last : last + 16],
        )


def scan(slot, patches, pixel, gain):
    rows, blocks, _ = pixel.shape
    edge = jax.ShapeDtypeStruct((rows // 2, 16, 128), jnp.float32)
    return pl.pallas_call(
        scan_kernel,
        out_shape=(jax.ShapeDtypeStruct((rows, 16 * blocks, 128), jnp.float32), edge, edge),
        in_specs=[smem()] + vmem(3),
        out_specs=tuple(vmem(3)),
    )(slot, patches, pixel, gain)


def project_kernel(
    slot_ref, line_ref, before_ref, after_ref, base_ref, pixel_ref, gain_ref, out_ref
):
    rows, blocks, _ = pixel_ref.shape
    half = rows // 2
    down = lax.broadcasted_iota(jnp.int32, (128, 128), 0)
    across = lax.broadcasted_iota(jnp.int32, (128, 128), 1)
    place = lax.broadcasted_iota(jnp.int32, (64, 128), 0)

    def one_row(d, before, after):
        base = jnp.broadcast_to(base_ref[d], (128, 256))
        turned = pltpu.roll(base, 0, 1, stride=1, stride_axis=0)
        near, far = turned[:, :128], turned[:, 128:]
        band = jnp.concatenate(
            [jnp.where(down > across, far, 0.0), near, jnp.where(down < across, far, 0.0)], axis=0
        )
        band_top, band_low = halves(band)
        cells = jnp.concatenate([before, line_ref[d], after], axis=0)
        top, low = halves(cells)
        wide_top = jnp.concatenate(
            [top[16 * o : 16 * (o + blocks)] for o in range(3)], axis=1
        )
        wide_low = jnp.concatenate(
            [low[16 * o : 16 * (o + blocks)] for o in range(3)], axis=1
        )
        filtered = (
            jnp.dot(wide_top, band_top, preferred_element_type=jnp.float32)
            + jnp.dot(wide_low, band_top, preferred_element_type=jnp.float32)
            + jnp.dot(wide_top, band_low, preferred_element_type=jnp.float32)
        )
        pixels, gains = pixel_ref[d], gain_ref[d]
        for j in range(blocks):
            gain = jnp.broadcast_to(gains[j : j + 1], (16, 128))
            pixel = jnp.broadcast_to(pixels[j : j + 1], (64, 128))
            hot = jnp.where(place == pixel, 1.0, 0.0).astype(jnp.bfloat16)
            both = jnp.concatenate(halves(filtered[16 * j : 16 * j + 16] * gain), axis=0)
            added = lax.dot_general(
                both, hot, (((1,), (1,)), ((), ())), preferred_element_type=jnp.float32
            )
            added = added[:16] + added[16:]
            out_ref[slot_ref[d * blocks + j]] = jnp.concatenate([added[:8], added[8:]], axis=1)

    @pl.loop(0, half)
    def _(d):
        before, after = before_ref[d], after_ref[d]
        one_row(d, before, after)
        one_row(d + half, pltpu.roll(before, 64, 1), pltpu.roll(after, 64, 1))


def project(slot, line, before, after, base, pixel, gain):
    rows, blocks, _ = pixel.shape
    return pl.pallas_call(
        project_kernel,
        out_shape=jax.ShapeDtypeStruct((rows * blocks, 8, 128), jnp.float32),
        in_specs=[smem()] + vmem(6),
        out_specs=vmem(1)[0],
        compiler_params=pltpu.CompilerParams(vmem_limit_bytes=40 * 1024 * 1024),
    )(slot, line, before, after, base, pixel, gain)


def share_kernel(spans, devices, part_ref, out_ref, held, send_sem, recv_sem):
    me = lax.axis_index("det") * spans + lax.axis_index("tm")
    barrier = pltpu.get_barrier_semaphore()

    def place(step):
        peer = lax.rem(me + step, devices)
        return (peer // spans, lax.rem(peer, spans))

    def copy_to(step):
        return pltpu.make_async_remote_copy(
            src_ref=part_ref,
            dst_ref=held.at[step],
            send_sem=send_sem.at[step],
            recv_sem=recv_sem.at[step],
            device_id=place(step),
            device_id_type=pl.DeviceIdType.MESH,
        )

    @pl.loop(1, devices)
    def _(step):
        pl.semaphore_signal(
            barrier, inc=1, device_id=place(step), device_id_type=pl.DeviceIdType.MESH
        )

    pl.semaphore_wait(barrier, devices - 1)

    @pl.loop(1, devices)
    def _(step):
        copy_to(step).start()

    held[0] = part_ref[...]

    @pl.loop(1, devices)
    def _(step):
        copy_to(step).wait()

    out_ref[...] = jnp.sum(held[...], axis=0)


def sum_everywhere(part, spans, devices):
    return pl.pallas_call(
        functools.partial(share_kernel, spans, devices),
        out_shape=jax.ShapeDtypeStruct(part.shape, jnp.float32),
        in_specs=[pl.BlockSpec(memory_space=pltpu.VMEM)],
        out_specs=pl.BlockSpec(memory_space=pltpu.VMEM),
        scratch_shapes=[
            pltpu.VMEM((devices,) + part.shape, jnp.float32),
            pltpu.SemaphoreType.DMA((devices,)),
            pltpu.SemaphoreType.DMA((devices,)),
        ],
        compiler_params=pltpu.CompilerParams(collective_id=0, has_side_effects=True),
    )(part)


def per_device(
    iterate, residual, direction, precond, patch_ids, pixel_in, weights, filter_diag, filter_band
):
    probes = iterate.shape[0]
    det_rows, time_blocks = patch_ids.shape
    half_band = filter_band.shape[1]
    groups = lax.axis_size("det")
    spans = lax.axis_size("tm")
    devices = groups * spans
    blocks = det_rows * time_blocks
    per_owner = blocks // devices
    own_patches = iterate.shape[1] // PX
    patch_flat = patch_ids.reshape(blocks)
    owners = patch_flat // own_patches
    numbers = jnp.arange(blocks, dtype=jnp.int32)
    earlier = (owners[:, None] == owners[None, :]) & (numbers[None, :] < numbers[:, None])
    slot = owners * per_owner + jnp.sum(earlier.astype(jnp.int32), axis=1)
    requests = jnp.sum(
        jnp.where(numbers[:, None] == slot[None, :], (patch_flat % own_patches)[None, :], 0), axis=1
    ).reshape(devices, per_owner)
    asked = lax.all_to_all(requests, ("det", "tm"), split_axis=0, concat_axis=0, tiled=True)
    asked = asked.reshape(blocks)
    table = (
        direction.reshape(2, 8, own_patches, PX).transpose(2, 1, 0, 3).reshape(own_patches, 8, 128)
    )
    served = serve(asked, table).reshape(devices, per_owner, 8, 128)
    fetched = lax.all_to_all(served, ("det", "tm"), split_axis=0, concat_axis=0, tiled=True)
    pixels = pixel_in.reshape(det_rows, time_blocks, 128)
    gains = weights.reshape(det_rows, time_blocks, 128)
    line, head, tail = scan(slot, fetched.reshape(blocks, 8, 128), pixels, gains)
    before = lax.ppermute(tail, "tm", [(i, i + 1) for i in range(spans - 1)])
    after = lax.ppermute(head, "tm", [(i + 1, i) for i in range(spans - 1)])
    base = jnp.concatenate(
        [
            filter_diag[:, None],
            filter_band,
            jnp.zeros((det_rows, 255 - 2 * half_band), jnp.float32),
            filter_band[:, ::-1],
        ],
        axis=1,
    )[:, None, :]
    parts = project(slot, line, before, after, base, pixels, gains)
    collected = lax.all_to_all(
        parts.reshape(devices, per_owner, 8, 128),
        ("det", "tm"),
        split_axis=0,
        concat_axis=0,
        tiled=True,
    ).reshape(blocks, 8, 128)
    image_map = (
        gather_up(asked, collected, own_patches)
        .reshape(own_patches, 8, 2, PX)
        .transpose(2, 1, 0, 3)
        .reshape(probes, own_patches * PX)
    )
    lean = precond * residual
    drop = precond * image_map
    sums = jnp.stack(
        [
            jnp.sum(residual * lean, axis=1),
            jnp.sum(direction * image_map, axis=1),
            jnp.sum(image_map * lean, axis=1),
            jnp.sum(image_map * drop, axis=1),
        ]
    )
    part = jnp.pad(sums, ((0, 4), (0, 128 - probes)))
    total = sum_everywhere(part, spans, devices)
    norm_old, curvature, cross, square = (total[i, :probes] for i in range(4))
    step_size = norm_old / curvature
    norm_new = norm_old - step_size * (2.0 * cross - step_size * square)
    new_iterate = iterate + step_size[:, None] * direction
    new_residual = residual - step_size[:, None] * image_map
    scaled = precond * new_residual
    new_direction = scaled + (norm_new / norm_old)[:, None] * direction
    return (new_iterate, new_residual, new_direction)


def solution(mesh):
    in_specs = (
        P(None, ("det", "tm")),
        P(None, ("det", "tm")),
        P(None, ("det", "tm")),
        P(("det", "tm")),
        P("det", "tm"),
        P("det", "tm"),
        P("det", "tm"),
        P("det"),
        P("det", None),
    )
    out_specs = (P(None, ("det", "tm")), P(None, ("det", "tm")), P(None, ("det", "tm")))
    return jax.shard_map(
        per_device, mesh=mesh, in_specs=in_specs, out_specs=out_specs, check_vma=False
    )
```

```python
import functools
import math

import jax
import jax.numpy as jnp
from jax import lax
from jax.experimental import pallas as pl
from jax.experimental.pallas import tpu as pltpu
from jax.sharding import PartitionSpec as P

PX = 64


def halves(values):
    top = values.astype(jnp.bfloat16)
    return top, (values - top.astype(jnp.float32)).astype(jnp.bfloat16)


def vmem(count):
    return [pl.BlockSpec(memory_space=pltpu.VMEM)] * count


def smem():
    return pl.BlockSpec(memory_space=pltpu.SMEM)


def peers_of(spans, devices):
    me = lax.axis_index("det") * spans + lax.axis_index("tm")
    stride = spans + 1 if math.gcd(spans + 1, devices) == 1 else 1

    def ahead(step):
        return lax.rem(me + step * stride, devices)

    def behind(step):
        return lax.rem(me + (devices - step) * stride, devices)

    def place(peer):
        return (peer // spans, lax.rem(peer, spans))

    return me, ahead, behind, place


def remote(src, dst, sent, got, device):
    return pltpu.make_async_remote_copy(
        src_ref=src,
        dst_ref=dst,
        send_sem=sent,
        recv_sem=got,
        device_id=device,
        device_id_type=pl.DeviceIdType.MESH,
    )


def greet(devices, ahead, place):
    barrier = pltpu.get_barrier_semaphore()

    @pl.loop(1, devices)
    def _(step):
        pl.semaphore_signal(
            barrier, inc=1, device_id=place(ahead(step)), device_id_type=pl.DeviceIdType.MESH
        )

    pl.semaphore_wait(barrier, devices - 1)


def fetch_kernel(
    spans, devices, ask_ref, table_ref, asked_ref, out_ref,
    served, numbers, ask_sent, ask_got, sent, got, local,
):
    me, ahead, behind, place = peers_of(spans, devices)
    per_owner = out_ref.shape[1]
    greet(devices, ahead, place)

    def ask(step, slot):
        peer = ahead(step)
        return remote(
            ask_ref.at[peer], asked_ref.at[slot], ask_sent.at[step], ask_got.at[step], place(peer)
        )

    def give(step, slot):
        peer = ahead(step)
        return remote(
            served.at[peer], out_ref.at[slot], sent.at[step], got.at[step], place(peer)
        )

    @pl.loop(1, devices)
    def _(step):
        ask(step, me).start()

    asked_ref[me] = ask_ref[me]

    @pl.loop(1, devices)
    def _(step):
        ask(step, behind(step)).wait_recv()

    move = pltpu.make_async_copy(asked_ref, numbers, local)
    move.start()
    move.wait()

    @pl.loop(1, devices)
    def _(step):
        peer = ahead(step)
        for i in range(per_owner):
            served[peer, i] = table_ref[numbers[peer, 0, i]]
        give(step, me).start()

    for i in range(per_owner):
        out_ref[me, i] = table_ref[numbers[me, 0, i]]

    @pl.loop(1, devices)
    def _(step):
        ask(step, me).wait_send()
        give(step, me).wait_send()
        give(step, behind(step)).wait_recv()


def fetch(ask, table, per_owner, spans, devices):
    return pl.pallas_call(
        functools.partial(fetch_kernel, spans, devices),
        out_shape=(
            jax.ShapeDtypeStruct(ask.shape, jnp.int32),
            jax.ShapeDtypeStruct((devices, per_owner, 8, 128), jnp.float32),
        ),
        in_specs=vmem(2),
        out_specs=tuple(vmem(2)),
        scratch_shapes=[
            pltpu.VMEM((devices, per_owner, 8, 128), jnp.float32),
            pltpu.SMEM(ask.shape, jnp.int32),
        ]
        + [pltpu.SemaphoreType.DMA((devices,))] * 4
        + [pltpu.SemaphoreType.DMA],
        compiler_params=pltpu.CompilerParams(
            collective_id=1, has_side_effects=True, vmem_limit_bytes=32 * 1024 * 1024
        ),
    )(ask, table)


def swap_kernel(spans, devices, part_ref, out_ref, sent, got):
    me, ahead, behind, place = peers_of(spans, devices)
    greet(devices, ahead, place)

    def give(step, slot):
        peer = ahead(step)
        return remote(
            part_ref.at[peer], out_ref.at[slot], sent.at[step], got.at[step], place(peer)
        )

    @pl.loop(1, devices)
    def _(step):
        give(step, me).start()

    out_ref[me] = part_ref[me]

    @pl.loop(1, devices)
    def _(step):
        give(step, me).wait_send()
        give(step, behind(step)).wait_recv()


def swap(parts, spans, devices):
    return pl.pallas_call(
        functools.partial(swap_kernel, spans, devices),
        out_shape=jax.ShapeDtypeStruct(parts.shape, jnp.float32),
        in_specs=vmem(1),
        out_specs=vmem(1)[0],
        scratch_shapes=[pltpu.SemaphoreType.DMA((devices,))] * 2,
        compiler_params=pltpu.CompilerParams(
            collective_id=2, has_side_effects=True, vmem_limit_bytes=32 * 1024 * 1024
        ),
    )(parts)


def gather_up_kernel(asked_ref, parts_ref, out_ref):
    out_ref[...] = jnp.zeros_like(out_ref)

    @pl.loop(0, parts_ref.shape[0], step=8)
    def _(first):
        for i in range(8):
            row = asked_ref[first + i]
            out_ref[row] = out_ref[row] + parts_ref[first + i]


def gather_up(asked, parts, rows):
    return pl.pallas_call(
        gather_up_kernel,
        out_shape=jax.ShapeDtypeStruct((rows,) + parts.shape[1:], jnp.float32),
        in_specs=[smem()] + vmem(1),
        out_specs=vmem(1)[0],
    )(asked, parts)


def scan_kernel(slot_ref, patches_ref, pixel_ref, gain_ref, line_ref, head_ref, tail_ref):
    rows, blocks, _ = pixel_ref.shape
    half = rows // 2
    left = lax.broadcasted_iota(jnp.int32, (16, 128), 1) < 64

    def one_row(d):
        pixels, gains = pixel_ref[d], gain_ref[d]
        for j in range(blocks):
            pixel = jnp.broadcast_to(pixels[j : j + 1], (8, 128))
            gain = jnp.broadcast_to(gains[j : j + 1], (8, 128))
            patch = patches_ref[slot_ref[d * blocks + j]]
            line_ref[d, 16 * j : 16 * j + 8] = (
                jnp.take_along_axis(patch, pixel, axis=1) * gain
            )
            line_ref[d, 16 * j + 8 : 16 * j + 16] = (
                jnp.take_along_axis(patch, pixel + 64, axis=1) * gain
            )

    @pl.loop(0, half)
    def _(d):
        one_row(d)
        one_row(d + half)
        last = 16 * (blocks - 1)
        head_ref[d] = jnp.where(
            left, line_ref[d, 0:16], pltpu.roll(line_ref[d + half, 0:16], 64, 1)
        )
        tail_ref[d] = jnp.where(
            left,
            pltpu.roll(line_ref[d + half, last : last + 16], 64, 1),
            line_ref[d, last : last + 16],
        )


def scan(slot, patches, pixel, gain):
    rows, blocks, _ = pixel.shape
    edge = jax.ShapeDtypeStruct((rows // 2, 16, 128), jnp.float32)
    return pl.pallas_call(
        scan_kernel,
        out_shape=(jax.ShapeDtypeStruct((rows, 16 * blocks, 128), jnp.float32), edge, edge),
        in_specs=[smem()] + vmem(3),
        out_specs=tuple(vmem(3)),
    )(slot, patches, pixel, gain)


def project_kernel(
    slot_ref, line_ref, before_ref, after_ref, base_ref, pixel_ref, gain_ref, out_ref
):
    rows, blocks, _ = pixel_ref.shape
    half = rows // 2
    down = lax.broadcasted_iota(jnp.int32, (128, 128), 0)
    across = lax.broadcasted_iota(jnp.int32, (128, 128), 1)
    place = lax.broadcasted_iota(jnp.int32, (64, 128), 0)

    def one_row(d, before, after):
        base = jnp.broadcast_to(base_ref[d], (128, 256))
        turned = pltpu.roll(base, 0, 1, stride=1, stride_axis=0)
        near, far = turned[:, :128], turned[:, 128:]
        band = jnp.concatenate(
            [jnp.where(down > across, far, 0.0), near, jnp.where(down < across, far, 0.0)], axis=0
        )
        band_top, band_low = halves(band)
        cells = jnp.concatenate([before, line_ref[d], after], axis=0)
        top, low = halves(cells)
        wide_top = jnp.concatenate(
            [top[16 * o : 16 * (o + blocks)] for o in range(3)], axis=1
        )
        wide_low = jnp.concatenate(
            [low[16 * o : 16 * (o + blocks)] for o in range(3)], axis=1
        )
        filtered = (
            jnp.dot(wide_top, band_top, preferred_element_type=jnp.float32)
            + jnp.dot(wide_low, band_top, preferred_element_type=jnp.float32)
            + jnp.dot(wide_top, band_low, preferred_element_type=jnp.float32)
        )
        pixels, gains = pixel_ref[d], gain_ref[d]
        for j in range(blocks):
            gain = jnp.broadcast_to(gains[j : j + 1], (16, 128))
            pixel = jnp.broadcast_to(pixels[j : j + 1], (64, 128))
            hot = jnp.where(place == pixel, 1.0, 0.0).astype(jnp.bfloat16)
            both = jnp.concatenate(halves(filtered[16 * j : 16 * j + 16] * gain), axis=0)
            added = lax.dot_general(
                both, hot, (((1,), (1,)), ((), ())), preferred_element_type=jnp.float32
            )
            added = added[:16] + added[16:]
            out_ref[slot_ref[d * blocks + j]] = jnp.concatenate([added[:8], added[8:]], axis=1)

    @pl.loop(0, half)
    def _(d):
        before, after = before_ref[d], after_ref[d]
        one_row(d, before, after)
        one_row(d + half, pltpu.roll(before, 64, 1), pltpu.roll(after, 64, 1))


def project(slot, line, before, after, base, pixel, gain):
    rows, blocks, _ = pixel.shape
    return pl.pallas_call(
        project_kernel,
        out_shape=jax.ShapeDtypeStruct((rows * blocks, 8, 128), jnp.float32),
        in_specs=[smem()] + vmem(6),
        out_specs=vmem(1)[0],
        compiler_params=pltpu.CompilerParams(vmem_limit_bytes=40 * 1024 * 1024),
    )(slot, line, before, after, base, pixel, gain)


def share_kernel(spans, devices, part_ref, out_ref, held, send_sem, recv_sem):
    me = lax.axis_index("det") * spans + lax.axis_index("tm")
    barrier = pltpu.get_barrier_semaphore()

    def place(step):
        peer = lax.rem(me + step, devices)
        return (peer // spans, lax.rem(peer, spans))

    def copy_to(step):
        return pltpu.make_async_remote_copy(
            src_ref=part_ref,
            dst_ref=held.at[step],
            send_sem=send_sem.at[step],
            recv_sem=recv_sem.at[step],
            device_id=place(step),
            device_id_type=pl.DeviceIdType.MESH,
        )

    @pl.loop(1, devices)
    def _(step):
        pl.semaphore_signal(
            barrier, inc=1, device_id=place(step), device_id_type=pl.DeviceIdType.MESH
        )

    pl.semaphore_wait(barrier, devices - 1)

    @pl.loop(1, devices)
    def _(step):
        copy_to(step).start()

    held[0] = part_ref[...]

    @pl.loop(1, devices)
    def _(step):
        copy_to(step).wait()

    out_ref[...] = jnp.sum(held[...], axis=0)


def sum_everywhere(part, spans, devices):
    return pl.pallas_call(
        functools.partial(share_kernel, spans, devices),
        out_shape=jax.ShapeDtypeStruct(part.shape, jnp.float32),
        in_specs=[pl.BlockSpec(memory_space=pltpu.VMEM)],
        out_specs=pl.BlockSpec(memory_space=pltpu.VMEM),
        scratch_shapes=[
            pltpu.VMEM((devices,) + part.shape, jnp.float32),
            pltpu.SemaphoreType.DMA((devices,)),
            pltpu.SemaphoreType.DMA((devices,)),
        ],
        compiler_params=pltpu.CompilerParams(collective_id=0, has_side_effects=True),
    )(part)


def per_device(
    iterate, residual, direction, precond, patch_ids, pixel_in, weights, filter_diag, filter_band
):
    probes = iterate.shape[0]
    det_rows, time_blocks = patch_ids.shape
    half_band = filter_band.shape[1]
    groups = lax.axis_size("det")
    spans = lax.axis_size("tm")
    devices = groups * spans
    blocks = det_rows * time_blocks
    per_owner = blocks // devices
    own_patches = iterate.shape[1] // PX
    patch_flat = patch_ids.reshape(blocks)
    owners = patch_flat // own_patches
    numbers = jnp.arange(blocks, dtype=jnp.int32)
    earlier = (owners[:, None] == owners[None, :]) & (numbers[None, :] < numbers[:, None])
    slot = owners * per_owner + jnp.sum(earlier.astype(jnp.int32), axis=1)
    requests = jnp.sum(
        jnp.where(numbers[:, None] == slot[None, :], (patch_flat % own_patches)[None, :], 0), axis=1
    ).reshape(devices, per_owner)
    requests = jnp.pad(requests, ((0, 0), (0, 128 - per_owner)))[:, None, :]
    table = (
        direction.reshape(2, 8, own_patches, PX).transpose(2, 1, 0, 3).reshape(own_patches, 8, 128)
    )
    asked, fetched = fetch(requests, table, per_owner, spans, devices)
    asked = asked[:, 0, :per_owner].reshape(blocks)
    pixels = pixel_in.reshape(det_rows, time_blocks, 128)
    gains = weights.reshape(det_rows, time_blocks, 128)
    line, head, tail = scan(slot, fetched.reshape(blocks, 8, 128), pixels, gains)
    before = lax.ppermute(tail, "tm", [(i, i + 1) for i in range(spans - 1)])
    after = lax.ppermute(head, "tm", [(i + 1, i) for i in range(spans - 1)])
    base = jnp.concatenate(
        [
            filter_diag[:, None],
            filter_band,
            jnp.zeros((det_rows, 255 - 2 * half_band), jnp.float32),
            filter_band[:, ::-1],
        ],
        axis=1,
    )[:, None, :]
    parts = project(slot, line, before, after, base, pixels, gains)
    collected = swap(parts.reshape(devices, per_owner, 8, 128), spans, devices)
    collected = collected.reshape(blocks, 8, 128)
    image_map = (
        gather_up(asked, collected, own_patches)
        .reshape(own_patches, 8, 2, PX)
        .transpose(2, 1, 0, 3)
        .reshape(probes, own_patches * PX)
    )
    lean = precond * residual
    drop = precond * image_map
    sums = jnp.stack(
        [
            jnp.sum(residual * lean, axis=1),
            jnp.sum(direction * image_map, axis=1),
            jnp.sum(image_map * lean, axis=1),
            jnp.sum(image_map * drop, axis=1),
        ]
    )
    part = jnp.pad(sums, ((0, 4), (0, 128 - probes)))
    total = sum_everywhere(part, spans, devices)
    norm_old, curvature, cross, square = (total[i, :probes] for i in range(4))
    step_size = norm_old / curvature
    norm_new = norm_old - step_size * (2.0 * cross - step_size * square)
    new_iterate = iterate + step_size[:, None] * direction
    new_residual = residual - step_size[:, None] * image_map
    scaled = precond * new_residual
    new_direction = scaled + (norm_new / norm_old)[:, None] * direction
    return (new_iterate, new_residual, new_direction)


def solution(mesh):
    in_specs = (
        P(None, ("det", "tm")),
        P(None, ("det", "tm")),
        P(None, ("det", "tm")),
        P(("det", "tm")),
        P("det", "tm"),
        P("det", "tm"),
        P("det", "tm"),
        P("det"),
        P("det", None),
    )
    out_specs = (P(None, ("det", "tm")), P(None, ("det", "tm")), P(None, ("det", "tm")))
    return jax.shard_map(
        per_device, mesh=mesh, in_specs=in_specs, out_specs=out_specs, check_vma=False
    )
```

```python
import functools
import math

import jax
import jax.numpy as jnp
from jax import lax
from jax.experimental import pallas as pl
from jax.experimental.pallas import tpu as pltpu
from jax.sharding import PartitionSpec as P

PX = 64


def halves(values):
    top = values.astype(jnp.bfloat16)
    return top, (values - top.astype(jnp.float32)).astype(jnp.bfloat16)


def vmem(count):
    return [pl.BlockSpec(memory_space=pltpu.VMEM)] * count


def smem():
    return pl.BlockSpec(memory_space=pltpu.SMEM)


def peers_of(spans, devices):
    me = lax.axis_index("det") * spans + lax.axis_index("tm")
    stride = spans + 1 if math.gcd(spans + 1, devices) == 1 else 1

    def ahead(step):
        return lax.rem(me + step * stride, devices)

    def behind(step):
        return lax.rem(me + (devices - step) * stride, devices)

    def place(peer):
        return (peer // spans, lax.rem(peer, spans))

    return me, ahead, behind, place


def remote(src, dst, sent, got, device):
    return pltpu.make_async_remote_copy(
        src_ref=src,
        dst_ref=dst,
        send_sem=sent,
        recv_sem=got,
        device_id=device,
        device_id_type=pl.DeviceIdType.MESH,
    )


def greet(devices, ahead, place):
    barrier = pltpu.get_barrier_semaphore()

    @pl.loop(1, devices)
    def _(step):
        pl.semaphore_signal(
            barrier, inc=1, device_id=place(ahead(step)), device_id_type=pl.DeviceIdType.MESH
        )

    pl.semaphore_wait(barrier, devices - 1)


def fetch_kernel(
    spans, devices, ask_ref, table_ref, asked_ref, out_ref,
    served, numbers, ask_sent, ask_got, sent, got, local,
):
    me, ahead, behind, place = peers_of(spans, devices)
    per_owner = out_ref.shape[1]
    greet(devices, ahead, place)

    def ask(step, slot):
        peer = ahead(step)
        return remote(
            ask_ref.at[peer], asked_ref.at[slot], ask_sent.at[step], ask_got.at[step], place(peer)
        )

    def give(step, slot):
        peer = ahead(step)
        return remote(
            served.at[peer], out_ref.at[slot], sent.at[step], got.at[step], place(peer)
        )

    @pl.loop(1, devices)
    def _(step):
        ask(step, me).start()

    asked_ref[me] = ask_ref[me]

    @pl.loop(1, devices)
    def _(step):
        ask(step, behind(step)).wait_recv()

    move = pltpu.make_async_copy(asked_ref, numbers, local)
    move.start()
    move.wait()

    @pl.loop(1, devices)
    def _(step):
        peer = ahead(step)
        for i in range(per_owner):
            served[peer, i] = table_ref[numbers[peer, 0, i]]
        give(step, me).start()

    for i in range(per_owner):
        out_ref[me, i] = table_ref[numbers[me, 0, i]]

    @pl.loop(1, devices)
    def _(step):
        ask(step, me).wait_send()
        give(step, me).wait_send()
        give(step, behind(step)).wait_recv()


def fetch(ask, table, per_owner, spans, devices):
    return pl.pallas_call(
        functools.partial(fetch_kernel, spans, devices),
        out_shape=(
            jax.ShapeDtypeStruct(ask.shape, jnp.int32),
            jax.ShapeDtypeStruct((devices, per_owner, 8, 128), jnp.float32),
        ),
        in_specs=vmem(2),
        out_specs=tuple(vmem(2)),
        scratch_shapes=[
            pltpu.VMEM((devices, per_owner, 8, 128), jnp.float32),
            pltpu.SMEM(ask.shape, jnp.int32),
        ]
        + [pltpu.SemaphoreType.DMA((devices,))] * 4
        + [pltpu.SemaphoreType.DMA],
        compiler_params=pltpu.CompilerParams(
            collective_id=1, has_side_effects=True, vmem_limit_bytes=32 * 1024 * 1024
        ),
    )(ask, table)


def swap_kernel(spans, devices, part_ref, out_ref, sent, got):
    me, ahead, behind, place = peers_of(spans, devices)
    greet(devices, ahead, place)

    def give(step, slot):
        peer = ahead(step)
        return remote(
            part_ref.at[peer], out_ref.at[slot], sent.at[step], got.at[step], place(peer)
        )

    @pl.loop(1, devices)
    def _(step):
        give(step, me).start()

    out_ref[me] = part_ref[me]

    @pl.loop(1, devices)
    def _(step):
        give(step, me).wait_send()
        give(step, behind(step)).wait_recv()


def swap(parts, spans, devices):
    return pl.pallas_call(
        functools.partial(swap_kernel, spans, devices),
        out_shape=jax.ShapeDtypeStruct(parts.shape, jnp.float32),
        in_specs=vmem(1),
        out_specs=vmem(1)[0],
        scratch_shapes=[pltpu.SemaphoreType.DMA((devices,))] * 2,
        compiler_params=pltpu.CompilerParams(
            collective_id=2, has_side_effects=True, vmem_limit_bytes=32 * 1024 * 1024
        ),
    )(parts)


def gather_up_kernel(asked_ref, parts_ref, out_ref, *others):
    chains = (out_ref,) + others
    share = parts_ref.shape[0] // len(chains)
    for chain in chains:
        chain[...] = jnp.zeros_like(chain)

    @pl.loop(0, share, unroll=4)
    def _(i):
        for c, chain in enumerate(chains):
            row = asked_ref[c * share + i]
            chain[row] = chain[row] + parts_ref[c * share + i]

    total = out_ref[...]
    for chain in others:
        total = total + chain[...]
    out_ref[...] = total


def gather_up(asked, parts, rows):
    return pl.pallas_call(
        gather_up_kernel,
        out_shape=jax.ShapeDtypeStruct((rows,) + parts.shape[1:], jnp.float32),
        in_specs=[smem()] + vmem(1),
        out_specs=vmem(1)[0],
        scratch_shapes=[pltpu.VMEM((rows,) + parts.shape[1:], jnp.float32)] * 3,
    )(asked, parts)


def scan_kernel(slot_ref, patches_ref, pixel_ref, gain_ref, line_ref, head_ref, tail_ref):
    rows, blocks, _ = pixel_ref.shape
    half = rows // 2
    left = lax.broadcasted_iota(jnp.int32, (16, 128), 1) < 64

    def one_row(d):
        pixels, gains = pixel_ref[d], gain_ref[d]
        ends = []
        for j in range(blocks):
            pixel = jnp.broadcast_to(pixels[j : j + 1], (8, 128))
            gain = jnp.broadcast_to(gains[j : j + 1], (8, 128))
            patch = patches_ref[slot_ref[d * blocks + j]]
            upper = jnp.take_along_axis(patch, pixel, axis=1) * gain
            lower = jnp.take_along_axis(patch, pixel + 64, axis=1) * gain
            line_ref[d, 16 * j : 16 * j + 8] = upper
            line_ref[d, 16 * j + 8 : 16 * j + 16] = lower
            if j in (0, blocks - 1):
                ends.append(jnp.concatenate([upper, lower], axis=0))
        return ends[0], ends[-1]

    @pl.loop(0, half, unroll=2)
    def _(d):
        first, last = one_row(d)
        later_first, later_last = one_row(d + half)
        head_ref[d] = jnp.where(left, first, pltpu.roll(later_first, 64, 1))
        tail_ref[d] = jnp.where(left, pltpu.roll(later_last, 64, 1), last)


def scan(slot, patches, pixel, gain):
    rows, blocks, _ = pixel.shape
    edge = jax.ShapeDtypeStruct((rows // 2, 16, 128), jnp.float32)
    return pl.pallas_call(
        scan_kernel,
        out_shape=(jax.ShapeDtypeStruct((rows, 16 * blocks, 128), jnp.float32), edge, edge),
        in_specs=[smem()] + vmem(3),
        out_specs=tuple(vmem(3)),
    )(slot, patches, pixel, gain)


def project_kernel(
    slot_ref, line_ref, before_ref, after_ref, base_ref, pixel_ref, gain_ref, out_ref
):
    rows, blocks, _ = pixel_ref.shape
    half = rows // 2
    down = lax.broadcasted_iota(jnp.int32, (128, 128), 0)
    across = lax.broadcasted_iota(jnp.int32, (128, 128), 1)
    place = lax.broadcasted_iota(jnp.int32, (64, 128), 0)

    def one_row(d, before, after):
        base = jnp.broadcast_to(base_ref[d], (128, 256))
        turned = pltpu.roll(base, 0, 1, stride=1, stride_axis=0)
        near, far = turned[:, :128], turned[:, 128:]
        band = jnp.concatenate(
            [jnp.where(down > across, far, 0.0), near, jnp.where(down < across, far, 0.0)], axis=0
        )
        band_top, band_low = halves(band)
        cells = jnp.concatenate([before, line_ref[d], after], axis=0)
        top, low = halves(cells)
        wide_top = jnp.concatenate(
            [top[16 * o : 16 * (o + blocks)] for o in range(3)], axis=1
        )
        wide_low = jnp.concatenate(
            [low[16 * o : 16 * (o + blocks)] for o in range(3)], axis=1
        )
        filtered = (
            jnp.dot(wide_top, band_top, preferred_element_type=jnp.float32)
            + jnp.dot(wide_low, band_top, preferred_element_type=jnp.float32)
            + jnp.dot(wide_top, band_low, preferred_element_type=jnp.float32)
        )
        pixels, gains = pixel_ref[d], gain_ref[d]
        for j in range(blocks):
            gain = jnp.broadcast_to(gains[j : j + 1], (16, 128))
            pixel = jnp.broadcast_to(pixels[j : j + 1], (64, 128))
            hot = jnp.where(place == pixel, 1.0, 0.0).astype(jnp.bfloat16)
            both = jnp.concatenate(halves(filtered[16 * j : 16 * j + 16] * gain), axis=0)
            added = lax.dot_general(
                both, hot, (((1,), (1,)), ((), ())), preferred_element_type=jnp.float32
            )
            added = added[:16] + added[16:]
            out_ref[slot_ref[d * blocks + j]] = jnp.concatenate([added[:8], added[8:]], axis=1)

    @pl.loop(0, half, unroll=2)
    def _(d):
        before, after = before_ref[d], after_ref[d]
        one_row(d, before, after)
        one_row(d + half, pltpu.roll(before, 64, 1), pltpu.roll(after, 64, 1))


def project(slot, line, before, after, base, pixel, gain):
    rows, blocks, _ = pixel.shape
    return pl.pallas_call(
        project_kernel,
        out_shape=jax.ShapeDtypeStruct((rows * blocks, 8, 128), jnp.float32),
        in_specs=[smem()] + vmem(6),
        out_specs=vmem(1)[0],
        compiler_params=pltpu.CompilerParams(vmem_limit_bytes=40 * 1024 * 1024),
    )(slot, line, before, after, base, pixel, gain)


def factors_kernel(
    spans, devices, old_ref, way_ref, scale_ref, image_ref, out_ref, part, held, sent, got
):
    me, ahead, behind, place = peers_of(spans, devices)
    barrier = pltpu.get_barrier_semaphore()

    @pl.loop(1, devices)
    def _(step):
        pl.semaphore_signal(
            barrier, inc=1, device_id=place(ahead(step)), device_id_type=pl.DeviceIdType.MESH
        )

    image = image_ref[...]
    lean = scale_ref[...] * old_ref[...]
    columns = (
        jnp.sum(old_ref[...] * lean, axis=1, keepdims=True),
        jnp.sum(way_ref[...] * image, axis=1, keepdims=True),
        jnp.sum(image * lean, axis=1, keepdims=True),
        jnp.sum(image * (scale_ref[...] * image), axis=1, keepdims=True),
    )
    lane = lax.broadcasted_iota(jnp.int32, part.shape, 1)
    tile = jnp.zeros(part.shape, jnp.float32)
    for i, column in enumerate(columns):
        tile = jnp.where(lane == i, column, tile)
    part[...] = tile
    held[me] = tile
    pl.semaphore_wait(barrier, devices - 1)

    def give(step, slot):
        return remote(
            part, held.at[slot], sent.at[step], got.at[step], place(ahead(step))
        )

    @pl.loop(1, devices)
    def _(step):
        give(step, me).start()

    @pl.loop(1, devices)
    def _(step):
        give(step, me).wait_send()
        give(step, behind(step)).wait_recv()

    total = jnp.sum(held[...], axis=0)
    norm_old, curvature, cross, square = (total[:, i : i + 1] for i in range(4))
    step_size = norm_old / curvature
    norm_new = norm_old - step_size * (2.0 * cross - step_size * square)
    out_ref[...] = jnp.where(lane == 0, step_size, norm_new / norm_old)


def factors(residual, direction, precond, image, spans, devices):
    tile = (residual.shape[0], 128)
    return pl.pallas_call(
        functools.partial(factors_kernel, spans, devices),
        out_shape=jax.ShapeDtypeStruct(tile, jnp.float32),
        in_specs=vmem(4),
        out_specs=vmem(1)[0],
        scratch_shapes=[
            pltpu.VMEM(tile, jnp.float32),
            pltpu.VMEM((devices,) + tile, jnp.float32),
            pltpu.SemaphoreType.DMA((devices,)),
            pltpu.SemaphoreType.DMA((devices,)),
        ],
        compiler_params=pltpu.CompilerParams(
            collective_id=0, has_side_effects=True, vmem_limit_bytes=32 * 1024 * 1024
        ),
    )(residual, direction, precond, image)


def per_device(
    iterate, residual, direction, precond, patch_ids, pixel_in, weights, filter_diag, filter_band
):
    probes = iterate.shape[0]
    det_rows, time_blocks = patch_ids.shape
    half_band = filter_band.shape[1]
    groups = lax.axis_size("det")
    spans = lax.axis_size("tm")
    devices = groups * spans
    blocks = det_rows * time_blocks
    per_owner = blocks // devices
    own_patches = iterate.shape[1] // PX
    patch_flat = patch_ids.reshape(blocks)
    owners = patch_flat // own_patches
    numbers = jnp.arange(blocks, dtype=jnp.int32)
    earlier = (owners[:, None] == owners[None, :]) & (numbers[None, :] < numbers[:, None])
    slot = owners * per_owner + jnp.sum(earlier.astype(jnp.int32), axis=1)
    requests = jnp.sum(
        jnp.where(numbers[:, None] == slot[None, :], (patch_flat % own_patches)[None, :], 0), axis=1
    ).reshape(devices, per_owner)
    requests = jnp.pad(requests, ((0, 0), (0, 128 - per_owner)))[:, None, :]
    table = (
        direction.reshape(2, 8, own_patches, PX).transpose(2, 1, 0, 3).reshape(own_patches, 8, 128)
    )
    asked, fetched = fetch(requests, table, per_owner, spans, devices)
    asked = asked[:, 0, :per_owner].reshape(blocks)
    pixels = pixel_in.reshape(det_rows, time_blocks, 128)
    gains = weights.reshape(det_rows, time_blocks, 128)
    line, head, tail = scan(slot, fetched.reshape(blocks, 8, 128), pixels, gains)
    before = lax.ppermute(tail, "tm", [(i, i + 1) for i in range(spans - 1)])
    after = lax.ppermute(head, "tm", [(i + 1, i) for i in range(spans - 1)])
    base = jnp.concatenate(
        [
            filter_diag[:, None],
            filter_band,
            jnp.zeros((det_rows, 255 - 2 * half_band), jnp.float32),
            filter_band[:, ::-1],
        ],
        axis=1,
    )[:, None, :]
    parts = project(slot, line, before, after, base, pixels, gains)
    collected = swap(parts.reshape(devices, per_owner, 8, 128), spans, devices)
    collected = collected.reshape(blocks, 8, 128)
    image_map = (
        gather_up(asked, collected, own_patches)
        .reshape(own_patches, 8, 2, PX)
        .transpose(2, 1, 0, 3)
        .reshape(probes, own_patches * PX)
    )
    factor = factors(residual, direction, precond[None, :], image_map, spans, devices)
    step_size, ratio = factor[:, 0:1], factor[:, 1:2]
    new_iterate = iterate + step_size * direction
    new_residual = residual - step_size * image_map
    new_direction = precond * new_residual + ratio * direction
    return (new_iterate, new_residual, new_direction)


def solution(mesh):
    in_specs = (
        P(None, ("det", "tm")),
        P(None, ("det", "tm")),
        P(None, ("det", "tm")),
        P(("det", "tm")),
        P("det", "tm"),
        P("det", "tm"),
        P("det", "tm"),
        P("det"),
        P("det", None),
    )
    out_specs = (P(None, ("det", "tm")), P(None, ("det", "tm")), P(None, ("det", "tm")))
    return jax.shard_map(
        per_device, mesh=mesh, in_specs=in_specs, out_specs=out_specs, check_vma=False
    )
```

```python
import functools
import math

import jax
import jax.numpy as jnp
from jax import lax
from jax.experimental import pallas as pl
from jax.experimental.pallas import tpu as pltpu
from jax.sharding import PartitionSpec as P

PX = 64


def halves(values):
    top = values.astype(jnp.bfloat16)
    return top, (values - top.astype(jnp.float32)).astype(jnp.bfloat16)


def vmem(count):
    return [pl.BlockSpec(memory_space=pltpu.VMEM)] * count


def smem():
    return pl.BlockSpec(memory_space=pltpu.SMEM)


def peers_of(spans, devices):
    me = lax.axis_index("det") * spans + lax.axis_index("tm")
    stride = spans + 1 if math.gcd(spans + 1, devices) == 1 else 1

    def ahead(step):
        return lax.rem(me + step * stride, devices)

    def behind(step):
        return lax.rem(me + (devices - step) * stride, devices)

    def place(peer):
        return (peer // spans, lax.rem(peer, spans))

    return me, ahead, behind, place


def remote(src, dst, sent, got, device):
    return pltpu.make_async_remote_copy(
        src_ref=src,
        dst_ref=dst,
        send_sem=sent,
        recv_sem=got,
        device_id=device,
        device_id_type=pl.DeviceIdType.MESH,
    )


def greet(devices, ahead, place):
    barrier = pltpu.get_barrier_semaphore()

    @pl.loop(1, devices)
    def _(step):
        pl.semaphore_signal(
            barrier, inc=1, device_id=place(ahead(step)), device_id_type=pl.DeviceIdType.MESH
        )

    pl.semaphore_wait(barrier, devices - 1)


def fetch_kernel(
    spans, devices, slot_ref, ask_ref, table_ref, pixel_ref, gain_ref,
    asked_ref, line_ref, before_ref, after_ref,
    served, patches, numbers, head, tail,
    ask_sent, ask_got, sent, got, local, edge_sent, edge_got,
):
    me, ahead, behind, place = peers_of(spans, devices)
    per_owner = served.shape[1]
    rows, blocks, _ = pixel_ref.shape
    half = rows // 2
    greet(devices, ahead, place)

    def ask(step, slot):
        peer = ahead(step)
        return remote(
            ask_ref.at[peer], asked_ref.at[slot], ask_sent.at[step], ask_got.at[step], place(peer)
        )

    def give(step, slot):
        peer = ahead(step)
        return remote(
            served.at[peer],
            patches.at[pl.ds(slot * per_owner, per_owner)],
            sent.at[step],
            got.at[step],
            place(peer),
        )

    @pl.loop(1, devices)
    def _(step):
        ask(step, me).start()

    asked_ref[me] = ask_ref[me]

    @pl.loop(1, devices)
    def _(step):
        ask(step, behind(step)).wait_recv()

    move = pltpu.make_async_copy(asked_ref, numbers, local)
    move.start()
    move.wait()

    @pl.loop(1, devices)
    def _(step):
        peer = ahead(step)
        for i in range(per_owner):
            served[peer, i] = table_ref[numbers[peer, 0, i]]
        give(step, me).start()

    for i in range(per_owner):
        patches[me * per_owner + i] = table_ref[numbers[me, 0, i]]

    @pl.loop(1, devices)
    def _(step):
        ask(step, me).wait_send()
        give(step, me).wait_send()
        give(step, behind(step)).wait_recv()

    left = lax.broadcasted_iota(jnp.int32, (16, 128), 1) < 64

    def scan(d, wanted):
        pixels, gains = pixel_ref[d], gain_ref[d]
        made = []
        for j in wanted:
            pixel = jnp.broadcast_to(pixels[j : j + 1], (8, 128))
            gain = jnp.broadcast_to(gains[j : j + 1], (8, 128))
            patch = patches[slot_ref[d * blocks + j]]
            upper = jnp.take_along_axis(patch, pixel, axis=1) * gain
            lower = jnp.take_along_axis(patch, pixel + 64, axis=1) * gain
            line_ref[d, 16 * j : 16 * j + 8] = upper
            line_ref[d, 16 * j + 8 : 16 * j + 16] = lower
            made.append(jnp.concatenate([upper, lower], axis=0))
        return made

    @pl.loop(0, half)
    def _(d):
        first, last = scan(d, (0, blocks - 1))
        later_first, later_last = scan(d + half, (0, blocks - 1))
        head[d] = jnp.where(left, first, pltpu.roll(later_first, 64, 1))
        tail[d] = jnp.where(left, pltpu.roll(later_last, 64, 1), last)

    span = lax.axis_index("tm")
    group = lax.axis_index("det")
    forth = remote(
        tail, before_ref, edge_sent.at[0], edge_got.at[0],
        (group, lax.rem(span + 1, spans)),
    )
    back = remote(
        head, after_ref, edge_sent.at[1], edge_got.at[1],
        (group, lax.rem(span + spans - 1, spans)),
    )
    forth.start()
    back.start()

    @pl.loop(0, rows)
    def _(d):
        scan(d, range(1, blocks - 1))

    forth.wait()
    back.wait()

    @pl.when(span == 0)
    def _():
        before_ref[...] = jnp.zeros_like(before_ref)

    @pl.when(span == spans - 1)
    def _():
        after_ref[...] = jnp.zeros_like(after_ref)


def fetch(slot, ask, table, pixels, gains, per_owner, spans, devices):
    rows, blocks, _ = pixels.shape
    edge = (rows // 2, 16, 128)
    return pl.pallas_call(
        functools.partial(fetch_kernel, spans, devices),
        out_shape=(
            jax.ShapeDtypeStruct(ask.shape, jnp.int32),
            jax.ShapeDtypeStruct((rows, 16 * blocks, 128), jnp.float32),
            jax.ShapeDtypeStruct(edge, jnp.float32),
            jax.ShapeDtypeStruct(edge, jnp.float32),
        ),
        in_specs=[smem()] + vmem(4),
        out_specs=tuple(vmem(4)),
        scratch_shapes=[
            pltpu.VMEM((devices, per_owner, 8, 128), jnp.float32),
            pltpu.VMEM((devices * per_owner, 8, 128), jnp.float32),
            pltpu.SMEM(ask.shape, jnp.int32),
            pltpu.VMEM(edge, jnp.float32),
            pltpu.VMEM(edge, jnp.float32),
        ]
        + [pltpu.SemaphoreType.DMA((devices,))] * 4
        + [pltpu.SemaphoreType.DMA]
        + [pltpu.SemaphoreType.DMA((2,))] * 2,
        compiler_params=pltpu.CompilerParams(
            collective_id=1, has_side_effects=True, vmem_limit_bytes=32 * 1024 * 1024
        ),
    )(slot, ask, table, pixels, gains)


def swap_kernel(spans, devices, part_ref, out_ref, sent, got):
    me, ahead, behind, place = peers_of(spans, devices)
    greet(devices, ahead, place)

    def give(step, slot):
        peer = ahead(step)
        return remote(
            part_ref.at[peer], out_ref.at[slot], sent.at[step], got.at[step], place(peer)
        )

    @pl.loop(1, devices)
    def _(step):
        give(step, me).start()

    out_ref[me] = part_ref[me]

    @pl.loop(1, devices)
    def _(step):
        give(step, me).wait_send()
        give(step, behind(step)).wait_recv()


def swap(parts, spans, devices):
    return pl.pallas_call(
        functools.partial(swap_kernel, spans, devices),
        out_shape=jax.ShapeDtypeStruct(parts.shape, jnp.float32),
        in_specs=vmem(1),
        out_specs=vmem(1)[0],
        scratch_shapes=[pltpu.SemaphoreType.DMA((devices,))] * 2,
        compiler_params=pltpu.CompilerParams(
            collective_id=2, has_side_effects=True, vmem_limit_bytes=32 * 1024 * 1024
        ),
    )(parts)


def gather_up_kernel(asked_ref, parts_ref, out_ref, *others):
    chains = (out_ref,) + others
    share = parts_ref.shape[0] // len(chains)
    for chain in chains:
        chain[...] = jnp.zeros_like(chain)

    @pl.loop(0, share, unroll=4)
    def _(i):
        for c, chain in enumerate(chains):
            row = asked_ref[c * share + i]
            chain[row] = chain[row] + parts_ref[c * share + i]

    total = out_ref[...]
    for chain in others:
        total = total + chain[...]
    out_ref[...] = total


def gather_up(asked, parts, rows):
    return pl.pallas_call(
        gather_up_kernel,
        out_shape=jax.ShapeDtypeStruct((rows,) + parts.shape[1:], jnp.float32),
        in_specs=[smem()] + vmem(1),
        out_specs=vmem(1)[0],
        scratch_shapes=[pltpu.VMEM((rows,) + parts.shape[1:], jnp.float32)] * 3,
    )(asked, parts)


def project_kernel(
    slot_ref, line_ref, before_ref, after_ref, base_ref, pixel_ref, gain_ref, out_ref
):
    rows, blocks, _ = pixel_ref.shape
    half = rows // 2
    down = lax.broadcasted_iota(jnp.int32, (128, 128), 0)
    across = lax.broadcasted_iota(jnp.int32, (128, 128), 1)
    place = lax.broadcasted_iota(jnp.int32, (64, 128), 0)

    def one_row(d, before, after):
        base = jnp.broadcast_to(base_ref[d], (128, 256))
        turned = pltpu.roll(base, 0, 1, stride=1, stride_axis=0)
        near, far = turned[:, :128], turned[:, 128:]
        band = jnp.concatenate(
            [jnp.where(down > across, far, 0.0), near, jnp.where(down < across, far, 0.0)], axis=0
        )
        band_top, band_low = halves(band)
        cells = jnp.concatenate([before, line_ref[d], after], axis=0)
        top, low = halves(cells)
        wide_top = jnp.concatenate(
            [top[16 * o : 16 * (o + blocks)] for o in range(3)], axis=1
        )
        wide_low = jnp.concatenate(
            [low[16 * o : 16 * (o + blocks)] for o in range(3)], axis=1
        )
        filtered = (
            jnp.dot(wide_top, band_top, preferred_element_type=jnp.float32)
            + jnp.dot(wide_low, band_top, preferred_element_type=jnp.float32)
            + jnp.dot(wide_top, band_low, preferred_element_type=jnp.float32)
        )
        pixels, gains = pixel_ref[d], gain_ref[d]
        for j in range(blocks):
            gain = jnp.broadcast_to(gains[j : j + 1], (16, 128))
            pixel = jnp.broadcast_to(pixels[j : j + 1], (64, 128))
            hot = jnp.where(place == pixel, 1.0, 0.0).astype(jnp.bfloat16)
            both = jnp.concatenate(halves(filtered[16 * j : 16 * j + 16] * gain), axis=0)
            added = lax.dot_general(
                both, hot, (((1,), (1,)), ((), ())), preferred_element_type=jnp.float32
            )
            added = added[:16] + added[16:]
            out_ref[slot_ref[d * blocks + j]] = jnp.concatenate([added[:8], added[8:]], axis=1)

    @pl.loop(0, half, unroll=2)
    def _(d):
        before, after = before_ref[d], after_ref[d]
        one_row(d, before, after)
        one_row(d + half, pltpu.roll(before, 64, 1), pltpu.roll(after, 64, 1))


def project(slot, line, before, after, base, pixel, gain):
    rows, blocks, _ = pixel.shape
    return pl.pallas_call(
        project_kernel,
        out_shape=jax.ShapeDtypeStruct((rows * blocks, 8, 128), jnp.float32),
        in_specs=[smem()] + vmem(6),
        out_specs=vmem(1)[0],
        compiler_params=pltpu.CompilerParams(vmem_limit_bytes=40 * 1024 * 1024),
    )(slot, line, before, after, base, pixel, gain)


def factors_kernel(
    spans, devices, old_ref, way_ref, scale_ref, image_ref, out_ref, part, held, sent, got
):
    me, ahead, behind, place = peers_of(spans, devices)
    barrier = pltpu.get_barrier_semaphore()

    @pl.loop(1, devices)
    def _(step):
        pl.semaphore_signal(
            barrier, inc=1, device_id=place(ahead(step)), device_id_type=pl.DeviceIdType.MESH
        )

    image = image_ref[...]
    lean = scale_ref[...] * old_ref[...]
    columns = (
        jnp.sum(old_ref[...] * lean, axis=1, keepdims=True),
        jnp.sum(way_ref[...] * image, axis=1, keepdims=True),
        jnp.sum(image * lean, axis=1, keepdims=True),
        jnp.sum(image * (scale_ref[...] * image), axis=1, keepdims=True),
    )
    lane = lax.broadcasted_iota(jnp.int32, part.shape, 1)
    tile = jnp.zeros(part.shape, jnp.float32)
    for i, column in enumerate(columns):
        tile = jnp.where(lane == i, column, tile)
    part[...] = tile
    held[me] = tile
    pl.semaphore_wait(barrier, devices - 1)

    def give(step, slot):
        return remote(
            part, held.at[slot], sent.at[step], got.at[step], place(ahead(step))
        )

    @pl.loop(1, devices)
    def _(step):
        give(step, me).start()

    @pl.loop(1, devices)
    def _(step):
        give(step, me).wait_send()
        give(step, behind(step)).wait_recv()

    total = jnp.sum(held[...], axis=0)
    norm_old, curvature, cross, square = (total[:, i : i + 1] for i in range(4))
    step_size = norm_old / curvature
    norm_new = norm_old - step_size * (2.0 * cross - step_size * square)
    out_ref[...] = jnp.where(lane == 0, step_size, norm_new / norm_old)


def factors(residual, direction, precond, image, spans, devices):
    tile = (residual.shape[0], 128)
    return pl.pallas_call(
        functools.partial(factors_kernel, spans, devices),
        out_shape=jax.ShapeDtypeStruct(tile, jnp.float32),
        in_specs=vmem(4),
        out_specs=vmem(1)[0],
        scratch_shapes=[
            pltpu.VMEM(tile, jnp.float32),
            pltpu.VMEM((devices,) + tile, jnp.float32),
            pltpu.SemaphoreType.DMA((devices,)),
            pltpu.SemaphoreType.DMA((devices,)),
        ],
        compiler_params=pltpu.CompilerParams(
            collective_id=0, has_side_effects=True, vmem_limit_bytes=32 * 1024 * 1024
        ),
    )(residual, direction, precond, image)


def per_device(
    iterate, residual, direction, precond, patch_ids, pixel_in, weights, filter_diag, filter_band
):
    probes = iterate.shape[0]
    det_rows, time_blocks = patch_ids.shape
    half_band = filter_band.shape[1]
    groups = lax.axis_size("det")
    spans = lax.axis_size("tm")
    devices = groups * spans
    blocks = det_rows * time_blocks
    per_owner = blocks // devices
    own_patches = iterate.shape[1] // PX
    patch_flat = patch_ids.reshape(blocks)
    owners = patch_flat // own_patches
    numbers = jnp.arange(blocks, dtype=jnp.int32)
    earlier = (owners[:, None] == owners[None, :]) & (numbers[None, :] < numbers[:, None])
    slot = owners * per_owner + jnp.sum(earlier.astype(jnp.int32), axis=1)
    requests = jnp.sum(
        jnp.where(numbers[:, None] == slot[None, :], (patch_flat % own_patches)[None, :], 0), axis=1
    ).reshape(devices, per_owner)
    requests = jnp.pad(requests, ((0, 0), (0, 128 - per_owner)))[:, None, :]
    table = (
        direction.reshape(2, 8, own_patches, PX).transpose(2, 1, 0, 3).reshape(own_patches, 8, 128)
    )
    pixels = pixel_in.reshape(det_rows, time_blocks, 128)
    gains = weights.reshape(det_rows, time_blocks, 128)
    asked, line, before, after = fetch(
        slot, requests, table, pixels, gains, per_owner, spans, devices
    )
    asked = asked[:, 0, :per_owner].reshape(blocks)
    base = jnp.concatenate(
        [
            filter_diag[:, None],
            filter_band,
            jnp.zeros((det_rows, 255 - 2 * half_band), jnp.float32),
            filter_band[:, ::-1],
        ],
        axis=1,
    )[:, None, :]
    parts = project(slot, line, before, after, base, pixels, gains)
    collected = swap(parts.reshape(devices, per_owner, 8, 128), spans, devices)
    collected = collected.reshape(blocks, 8, 128)
    image_map = (
        gather_up(asked, collected, own_patches)
        .reshape(own_patches, 8, 2, PX)
        .transpose(2, 1, 0, 3)
        .reshape(probes, own_patches * PX)
    )
    factor = factors(residual, direction, precond[None, :], image_map, spans, devices)
    step_size, ratio = factor[:, 0:1], factor[:, 1:2]
    new_iterate = iterate + step_size * direction
    new_residual = residual - step_size * image_map
    new_direction = precond * new_residual + ratio * direction
    return (new_iterate, new_residual, new_direction)


def solution(mesh):
    in_specs = (
        P(None, ("det", "tm")),
        P(None, ("det", "tm")),
        P(None, ("det", "tm")),
        P(("det", "tm")),
        P("det", "tm"),
        P("det", "tm"),
        P("det", "tm"),
        P("det"),
        P("det", None),
    )
    out_specs = (P(None, ("det", "tm")), P(None, ("det", "tm")), P(None, ("det", "tm")))
    return jax.shard_map(
        per_device, mesh=mesh, in_specs=in_specs, out_specs=out_specs, check_vma=False
    )
```

```python
import functools
import math

import jax
import jax.numpy as jnp
from jax import lax
from jax.experimental import pallas as pl
from jax.experimental.pallas import tpu as pltpu
from jax.sharding import PartitionSpec as P

PX = 64


def halves(values):
    top = values.astype(jnp.bfloat16)
    return top, (values - top.astype(jnp.float32)).astype(jnp.bfloat16)


def vmem(count):
    return [pl.BlockSpec(memory_space=pltpu.VMEM)] * count


def smem():
    return pl.BlockSpec(memory_space=pltpu.SMEM)


def peers_of(spans, devices):
    me = lax.axis_index("det") * spans + lax.axis_index("tm")
    stride = spans + 1 if math.gcd(spans + 1, devices) == 1 else 1

    def ahead(step):
        return lax.rem(me + step * stride, devices)

    def behind(step):
        return lax.rem(me + (devices - step) * stride, devices)

    def place(peer):
        return (peer // spans, lax.rem(peer, spans))

    return me, ahead, behind, place


def remote(src, dst, sent, got, device):
    return pltpu.make_async_remote_copy(
        src_ref=src,
        dst_ref=dst,
        send_sem=sent,
        recv_sem=got,
        device_id=device,
        device_id_type=pl.DeviceIdType.MESH,
    )


def greet(devices, ahead, place):
    barrier = pltpu.get_barrier_semaphore()

    @pl.loop(1, devices)
    def _(step):
        pl.semaphore_signal(
            barrier, inc=1, device_id=place(ahead(step)), device_id_type=pl.DeviceIdType.MESH
        )

    pl.semaphore_wait(barrier, devices - 1)


def fetch_kernel(
    spans, devices, slot_ref, ask_ref, table_ref, pixel_ref, gain_ref,
    asked_ref, line_ref, before_ref, after_ref,
    served, patches, numbers, head, tail,
    ask_sent, ask_got, sent, got, local, edge_sent, edge_got,
):
    me, ahead, behind, place = peers_of(spans, devices)
    per_owner = served.shape[1]
    rows, blocks, _ = pixel_ref.shape
    half = rows // 2
    greet(devices, ahead, place)

    def ask(step, slot):
        peer = ahead(step)
        return remote(
            ask_ref.at[peer], asked_ref.at[slot], ask_sent.at[step], ask_got.at[step], place(peer)
        )

    def give(step, slot):
        peer = ahead(step)
        return remote(
            served.at[peer],
            patches.at[pl.ds(slot * per_owner, per_owner)],
            sent.at[step],
            got.at[step],
            place(peer),
        )

    @pl.loop(1, devices)
    def _(step):
        ask(step, me).start()

    asked_ref[me] = ask_ref[me]

    @pl.loop(1, devices)
    def _(step):
        ask(step, behind(step)).wait_recv()

    move = pltpu.make_async_copy(asked_ref, numbers, local)
    move.start()
    move.wait()

    @pl.loop(1, devices)
    def _(step):
        peer = ahead(step)
        for i in range(per_owner):
            served[peer, i] = table_ref[numbers[peer, 0, i]]
        give(step, me).start()

    for i in range(per_owner):
        patches[me * per_owner + i] = table_ref[numbers[me, 0, i]]

    @pl.loop(1, devices)
    def _(step):
        ask(step, me).wait_send()
        give(step, me).wait_send()
        give(step, behind(step)).wait_recv()

    left = lax.broadcasted_iota(jnp.int32, (16, 128), 1) < 64

    def scan(d, wanted):
        pixels, gains = pixel_ref[d], gain_ref[d]
        made = []
        for j in wanted:
            pixel = jnp.broadcast_to(pixels[j : j + 1], (8, 128))
            gain = jnp.broadcast_to(gains[j : j + 1], (8, 128))
            patch = patches[slot_ref[d * blocks + j]]
            upper = jnp.take_along_axis(patch, pixel, axis=1) * gain
            lower = jnp.take_along_axis(patch, pixel + 64, axis=1) * gain
            line_ref[d, 16 * j : 16 * j + 8] = upper
            line_ref[d, 16 * j + 8 : 16 * j + 16] = lower
            made.append(jnp.concatenate([upper, lower], axis=0))
        return made

    @pl.loop(0, half)
    def _(d):
        first, last = scan(d, (0, blocks - 1))
        later_first, later_last = scan(d + half, (0, blocks - 1))
        head[d] = jnp.where(left, first, pltpu.roll(later_first, 64, 1))
        tail[d] = jnp.where(left, pltpu.roll(later_last, 64, 1), last)

    span = lax.axis_index("tm")
    group = lax.axis_index("det")
    forth = remote(
        tail, before_ref, edge_sent.at[0], edge_got.at[0],
        (group, lax.rem(span + 1, spans)),
    )
    back = remote(
        head, after_ref, edge_sent.at[1], edge_got.at[1],
        (group, lax.rem(span + spans - 1, spans)),
    )
    forth.start()
    back.start()

    @pl.loop(0, rows)
    def _(d):
        scan(d, range(1, blocks - 1))

    forth.wait()
    back.wait()

    @pl.when(span == 0)
    def _():
        before_ref[...] = jnp.zeros_like(before_ref)

    @pl.when(span == spans - 1)
    def _():
        after_ref[...] = jnp.zeros_like(after_ref)


def fetch(slot, ask, table, pixels, gains, per_owner, spans, devices):
    rows, blocks, _ = pixels.shape
    edge = (rows // 2, 16, 128)
    return pl.pallas_call(
        functools.partial(fetch_kernel, spans, devices),
        out_shape=(
            jax.ShapeDtypeStruct(ask.shape, jnp.int32),
            jax.ShapeDtypeStruct((rows, 16 * blocks, 128), jnp.float32),
            jax.ShapeDtypeStruct(edge, jnp.float32),
            jax.ShapeDtypeStruct(edge, jnp.float32),
        ),
        in_specs=[smem()] + vmem(4),
        out_specs=tuple(vmem(4)),
        scratch_shapes=[
            pltpu.VMEM((devices, per_owner, 8, 128), jnp.float32),
            pltpu.VMEM((devices * per_owner, 8, 128), jnp.float32),
            pltpu.SMEM(ask.shape, jnp.int32),
            pltpu.VMEM(edge, jnp.float32),
            pltpu.VMEM(edge, jnp.float32),
        ]
        + [pltpu.SemaphoreType.DMA((devices,))] * 4
        + [pltpu.SemaphoreType.DMA]
        + [pltpu.SemaphoreType.DMA((2,))] * 2,
        compiler_params=pltpu.CompilerParams(
            collective_id=1, has_side_effects=True, vmem_limit_bytes=32 * 1024 * 1024
        ),
    )(slot, ask, table, pixels, gains)


def settle_kernel(
    spans, devices, part_ref, asked_ref, way_ref, old_ref, scale_ref,
    image_ref, out_ref, landed, mine, held, sent, got, sum_sent, sum_got,
):
    me, ahead, behind, place = peers_of(spans, devices)
    per_owner = part_ref.shape[0] // devices
    patches = way_ref.shape[0]
    greet(devices, ahead, place)

    def give(step, slot):
        peer = ahead(step)
        return remote(
            part_ref.at[pl.ds(peer * per_owner, per_owner)],
            landed.at[pl.ds(slot * per_owner, per_owner)],
            sent.at[step],
            got.at[step],
            place(peer),
        )

    def tell(step, slot):
        return remote(
            mine, held.at[slot], sum_sent.at[step], sum_got.at[step], place(ahead(step))
        )

    @pl.loop(1, devices)
    def _(step):
        give(step, me).start()

    for i in range(per_owner):
        landed[me * per_owner + i] = part_ref[me * per_owner + i]
    rows = lax.broadcasted_iota(jnp.int32, (patches, part_ref.shape[0]), 0)
    hot = jnp.where(rows == asked_ref[...], 1.0, 0.0).astype(jnp.bfloat16)
    scale = scale_ref[...]

    @pl.loop(1, devices)
    def _(step):
        give(step, me).wait_send()
        give(step, behind(step)).wait_recv()

    sums = [[], [], [], []]
    for r in range(8):
        top, low = halves(landed[:, r, :])
        image = jnp.dot(hot, top, preferred_element_type=jnp.float32) + jnp.dot(
            hot, low, preferred_element_type=jnp.float32
        )
        image_ref[:, r, :] = image
        old = old_ref[:, r, :]
        lean = scale * old
        terms = (old * lean, way_ref[:, r, :] * image, image * lean, image * (scale * image))
        for kept, term in zip(sums, terms):
            kept.append(jnp.sum(term, axis=0, keepdims=True))
    tile = jnp.concatenate([row for kept in sums for row in kept], axis=0)
    mine[...] = tile
    held[me] = tile

    @pl.loop(1, devices)
    def _(step):
        tell(step, me).start()

    @pl.loop(1, devices)
    def _(step):
        tell(step, me).wait_send()
        tell(step, behind(step)).wait_recv()

    total = jnp.sum(held[...], axis=0)
    lane = lax.broadcasted_iota(jnp.int32, total.shape, 1)
    sides = (
        jnp.sum(jnp.where(lane < 64, total, 0.0), axis=1, keepdims=True),
        jnp.sum(jnp.where(lane < 64, 0.0, total), axis=1, keepdims=True),
    )
    for i, side in enumerate(sides):
        norm_old, curvature, cross, square = (side[8 * q : 8 * q + 8] for q in range(4))
        step_size = norm_old / curvature
        norm_new = norm_old - step_size * (2.0 * cross - step_size * square)
        out_ref[8 * i : 8 * i + 8] = jnp.where(
            lane[:8] == 0, step_size, norm_new / norm_old
        )


def settle(parts, asked, way, old, scale, spans, devices):
    return pl.pallas_call(
        functools.partial(settle_kernel, spans, devices),
        out_shape=(
            jax.ShapeDtypeStruct(way.shape, jnp.float32),
            jax.ShapeDtypeStruct((16, 128), jnp.float32),
        ),
        in_specs=vmem(5),
        out_specs=tuple(vmem(2)),
        scratch_shapes=[
            pltpu.VMEM(parts.shape, jnp.float32),
            pltpu.VMEM((32, 128), jnp.float32),
            pltpu.VMEM((devices, 32, 128), jnp.float32),
        ]
        + [pltpu.SemaphoreType.DMA((devices,))] * 4,
        compiler_params=pltpu.CompilerParams(
            collective_id=2, has_side_effects=True, vmem_limit_bytes=32 * 1024 * 1024
        ),
    )(parts, asked, way, old, scale)


def project_kernel(
    slot_ref, line_ref, before_ref, after_ref, base_ref, pixel_ref, gain_ref, out_ref
):
    rows, blocks, _ = pixel_ref.shape
    half = rows // 2
    down = lax.broadcasted_iota(jnp.int32, (128, 128), 0)
    across = lax.broadcasted_iota(jnp.int32, (128, 128), 1)
    place = lax.broadcasted_iota(jnp.int32, (64, 128), 0)

    def one_row(d, before, after):
        base = jnp.broadcast_to(base_ref[d], (128, 256))
        turned = pltpu.roll(base, 0, 1, stride=1, stride_axis=0)
        near, far = turned[:, :128], turned[:, 128:]
        band = jnp.concatenate(
            [jnp.where(down > across, far, 0.0), near, jnp.where(down < across, far, 0.0)], axis=0
        )
        band_top, band_low = halves(band)
        cells = jnp.concatenate([before, line_ref[d], after], axis=0)
        top, low = halves(cells)
        wide_top = jnp.concatenate(
            [top[16 * o : 16 * (o + blocks)] for o in range(3)], axis=1
        )
        wide_low = jnp.concatenate(
            [low[16 * o : 16 * (o + blocks)] for o in range(3)], axis=1
        )
        filtered = (
            jnp.dot(wide_top, band_top, preferred_element_type=jnp.float32)
            + jnp.dot(wide_low, band_top, preferred_element_type=jnp.float32)
            + jnp.dot(wide_top, band_low, preferred_element_type=jnp.float32)
        )
        pixels, gains = pixel_ref[d], gain_ref[d]
        for j in range(blocks):
            gain = jnp.broadcast_to(gains[j : j + 1], (16, 128))
            pixel = jnp.broadcast_to(pixels[j : j + 1], (64, 128))
            hot = jnp.where(place == pixel, 1.0, 0.0).astype(jnp.bfloat16)
            both = jnp.concatenate(halves(filtered[16 * j : 16 * j + 16] * gain), axis=0)
            added = lax.dot_general(
                both, hot, (((1,), (1,)), ((), ())), preferred_element_type=jnp.float32
            )
            added = added[:16] + added[16:]
            out_ref[slot_ref[d * blocks + j]] = jnp.concatenate([added[:8], added[8:]], axis=1)

    @pl.loop(0, half, unroll=2)
    def _(d):
        before, after = before_ref[d], after_ref[d]
        one_row(d, before, after)
        one_row(d + half, pltpu.roll(before, 64, 1), pltpu.roll(after, 64, 1))


def project(slot, line, before, after, base, pixel, gain):
    rows, blocks, _ = pixel.shape
    return pl.pallas_call(
        project_kernel,
        out_shape=jax.ShapeDtypeStruct((rows * blocks, 8, 128), jnp.float32),
        in_specs=[smem()] + vmem(6),
        out_specs=vmem(1)[0],
        compiler_params=pltpu.CompilerParams(vmem_limit_bytes=40 * 1024 * 1024),
    )(slot, line, before, after, base, pixel, gain)


def per_device(
    iterate, residual, direction, precond, patch_ids, pixel_in, weights, filter_diag, filter_band
):
    probes = iterate.shape[0]
    det_rows, time_blocks = patch_ids.shape
    half_band = filter_band.shape[1]
    groups = lax.axis_size("det")
    spans = lax.axis_size("tm")
    devices = groups * spans
    blocks = det_rows * time_blocks
    per_owner = blocks // devices
    own_patches = iterate.shape[1] // PX
    patch_flat = patch_ids.reshape(blocks)
    owners = patch_flat // own_patches
    numbers = jnp.arange(blocks, dtype=jnp.int32)
    earlier = (owners[:, None] == owners[None, :]) & (numbers[None, :] < numbers[:, None])
    slot = owners * per_owner + jnp.sum(earlier.astype(jnp.int32), axis=1)
    requests = jnp.sum(
        jnp.where(numbers[:, None] == slot[None, :], (patch_flat % own_patches)[None, :], 0), axis=1
    ).reshape(devices, per_owner)
    requests = jnp.pad(requests, ((0, 0), (0, 128 - per_owner)))[:, None, :]

    def tiles(field):
        return (
            field.reshape(2, 8, own_patches, PX)
            .transpose(2, 1, 0, 3)
            .reshape(own_patches, 8, 128)
        )

    table = tiles(direction)
    scale = jnp.tile(precond.reshape(own_patches, PX), (1, 2))
    pixels = pixel_in.reshape(det_rows, time_blocks, 128)
    gains = weights.reshape(det_rows, time_blocks, 128)
    asked, line, before, after = fetch(
        slot, requests, table, pixels, gains, per_owner, spans, devices
    )
    asked = asked[:, 0, :per_owner].reshape(1, blocks)
    base = jnp.concatenate(
        [
            filter_diag[:, None],
            filter_band,
            jnp.zeros((det_rows, 255 - 2 * half_band), jnp.float32),
            filter_band[:, ::-1],
        ],
        axis=1,
    )[:, None, :]
    parts = project(slot, line, before, after, base, pixels, gains)
    image_tiles, factor = settle(parts, asked, table, tiles(residual), scale, spans, devices)
    image_map = (
        image_tiles
        .reshape(own_patches, 8, 2, PX)
        .transpose(2, 1, 0, 3)
        .reshape(probes, own_patches * PX)
    )
    step_size, ratio = factor[:, 0:1], factor[:, 1:2]
    new_iterate = iterate + step_size * direction
    new_residual = residual - step_size * image_map
    new_direction = precond * new_residual + ratio * direction
    return (new_iterate, new_residual, new_direction)


def solution(mesh):
    in_specs = (
        P(None, ("det", "tm")),
        P(None, ("det", "tm")),
        P(None, ("det", "tm")),
        P(("det", "tm")),
        P("det", "tm"),
        P("det", "tm"),
        P("det", "tm"),
        P("det"),
        P("det", None),
    )
    out_specs = (P(None, ("det", "tm")), P(None, ("det", "tm")), P(None, ("det", "tm")))
    return jax.shard_map(
        per_device, mesh=mesh, in_specs=in_specs, out_specs=out_specs, check_vma=False
    )
```
